256 devices in a mesh: section: 8 (over z), dom: 16 (over y, x), ens: 2 (over core).
Axes of the slice: x: 4, y: 4, z: 8, core: 2. Of those that a mesh axis runs over, the one named last changes fastest.
Arguments:
- members: bfloat16 [16, 2048, 512], P(('section', 'ens'), 'dom'), may hold values from -6 to 6
- layer_mats: bfloat16 [8, 6, 512, 512], P('section'), may hold values from -0.25 to 0.25
- biases: float32 [8, 2, 512], P('section'), may hold values from -3 to 3
- norm_gains: float32 [8, 2, 512], P('section'), may hold values from 0.25 to 1.75
- edge_blocks: int32 [16, 6], P('dom'), may hold values from 0 to 2
- edge_shift: int32 [16, 6], P('dom'), may hold values from 0 to 127
Outputs:
- final_state: bfloat16 [16, 2048, 512], P(('section', 'ens'), 'dom')
- ens_mean: float32 [2048, 512], P('dom')
The draws below stay inside these ranges and needn't reach their ends.
Inputs may be any that keep to these rules, and one draw needn't show every extreme that they name: `edge_blocks`: a frame of 1 block of the previous part (wrapping around), the part's own 1 block, then 1 block of the next part.
All inputs are finite; a program needn't handle non-finite values.
Results may differ from the reference program's by a relative error of at most 0.022.
Values may be sent and summed in bfloat16 or wider, within the bound.
A program may use at most 64 MiB of HBM per device.

```python
import jax
import jax.numpy as jnp
from jax import lax

D = 512
BLK = 128
HB = 1
SLOTS = 6
BD = 1
NODES = 2048
NBLK = 16
MEMBERS = 16
LAYERS = 8


def touch_ends(entries, stream_key, low, top_value):
    spot = [jax.random.randint(jax.random.fold_in(stream_key, axis), (), 0, length) for axis, length in enumerate(entries.shape)]
    widest = entries.shape.index(max(entries.shape))
    beside = spot[:widest] + [(spot[widest] + 1) % entries.shape[widest]] + spot[widest + 1:]
    return entries.at[tuple(spot)].set(low).at[tuple(beside)].set(top_value)


def shard_levels(stream_key, shape, cuts, least, high):
    factor_of = 1.0
    for axis_at, parts in cuts:
        steps = jax.random.uniform(jax.random.fold_in(jax.random.fold_in(stream_key, 6), axis_at), (parts,), jnp.float32, least / len(cuts), high / len(cuts))
        factor_of = factor_of * jnp.repeat(jnp.exp(steps), shape[axis_at] // parts).reshape((-1,) + (1,) * (len(shape) - 1 - axis_at))
    return factor_of


def scatter_about(own_key, dims, deviation, bound, shards=(), kind=jnp.bfloat16):
    entries = deviation * jax.random.normal(own_key, dims, jnp.float32)
    if shards:
        entries = entries * shard_levels(own_key, dims, shards, -0.22, 0.18)
    return jnp.clip(entries, -bound, bound).astype(kind)


def setup_inputs(seed: int = 0) -> dict:
    seeds = jax.random.split(jax.random.key(seed), 7)
    return {
        "members": scatter_about(seeds[0], (MEMBERS, NODES, D), 1.0, 6.0, ((0, 16), (1, 16))),
        "layer_mats": scatter_about(seeds[1], (LAYERS, 6, D, D), D ** -0.5, 0.25, ((0, 8),)),
        "biases": scatter_about(seeds[2], (LAYERS, 2, D), 0.5, 3.0, ((0, 8),), jnp.float32),
        "norm_gains": jnp.clip(1.0 + 0.15 * jax.random.normal(seeds[3], (LAYERS, 2, D), jnp.float32), 0.25, 1.75),
        "edge_blocks": touch_ends(jax.random.randint(seeds[4], (NBLK, SLOTS), 0, BD + 2 * HB), jax.random.fold_in(seeds[4], 1), 0, (BD + 2 * HB) - 1).astype(jnp.int32),
        "edge_shift": touch_ends(jax.random.randint(seeds[5], (NBLK, SLOTS), 0, BLK), jax.random.fold_in(seeds[5], 1), 0, BLK - 1).astype(jnp.int32),
    }


EPSILON = 1e-05

def layer_norm(values):
    average = lax.optimization_barrier(jnp.mean(values, axis=-1, keepdims=True))
    centred = values - average
    spread = lax.optimization_barrier(jnp.mean(centred * centred, axis=-1, keepdims=True))
    return centred * lax.rsqrt(spread + EPSILON)

def node_update(state, sender_terms, sender_rows, matrices, bias_pair, gain_pair):
    width_d = state.shape[-1]
    receiver_terms = jnp.dot(state, matrices[1], preferred_element_type=jnp.float32) + bias_pair[0]
    picked = jnp.take(sender_terms, sender_rows.reshape(-1), axis=0).reshape(sender_rows.shape + (width_d,))
    pre_act = picked.astype(jnp.float32) + receiver_terms[:, None, :]
    hidden = jax.nn.silu(pre_act).astype(jnp.bfloat16)
    edge_out = jnp.dot(hidden.reshape(-1, width_d), matrices[2], preferred_element_type=jnp.float32)
    edge_out = edge_out.reshape(hidden.shape)
    messages = lax.optimization_barrier(jnp.sum(layer_norm(edge_out) * gain_pair[0], axis=1)).astype(jnp.bfloat16)
    node_pre = jnp.dot(state, matrices[3], preferred_element_type=jnp.float32) + jnp.dot(messages, matrices[4], preferred_element_type=jnp.float32) + bias_pair[1]
    node_hidden = jax.nn.silu(node_pre).astype(jnp.bfloat16)
    node_out = jnp.dot(node_hidden, matrices[5], preferred_element_type=jnp.float32)
    return (state.astype(jnp.float32) + layer_norm(node_out) * gain_pair[1]).astype(jnp.bfloat16)

def reference(members, layer_mats, biases, norm_gains, edge_blocks, edge_shift):
    node_ids = jnp.arange(NODES, dtype=jnp.int32)
    block_ids = node_ids // BLK
    positions = node_ids % BLK
    owners = block_ids // BD
    frame_block = edge_blocks[block_ids]
    offsets = edge_shift[block_ids]
    global_block = (owners[:, None] * BD + frame_block - HB) % NBLK
    sender_rows = (global_block * BLK + (positions[:, None] + offsets) % BLK).astype(jnp.int32)

    def rollout(state):
        for layer_no in range(LAYERS):
            matrices = layer_mats[layer_no]
            sender_terms = jnp.dot(state, matrices[0], preferred_element_type=jnp.float32).astype(jnp.bfloat16)
            state = node_update(state, sender_terms, sender_rows, matrices, biases[layer_no], norm_gains[layer_no])
        return state
    final_state = lax.map(rollout, members)
    ens_mean = lax.optimization_barrier(jnp.sum(final_state.astype(jnp.float32), axis=0)) / MEMBERS
    return (final_state, ens_mean)
```

```python
import jax
import jax.numpy as jnp
from jax import lax
from jax.experimental import pallas as pl
from jax.experimental.pallas import tpu as pltpu
from jax.sharding import PartitionSpec as P

BLK = 128
EPSILON = 1e-05
CHUNKS = 2
LANES = 128
MESH = pl.DeviceIdType.MESH


def shifted(axis, by):
    devices = lax.axis_size(axis)
    return lax.rem(lax.axis_index(axis) + by + devices, devices)


def mm(a, b):
    return jnp.dot(a, b, preferred_element_type=jnp.float32)


def centred(w):
    w = w.astype(jnp.float32)
    return (w - jnp.mean(w, axis=-1, keepdims=True)).astype(jnp.bfloat16)


def twice_half_silu(u):
    return u + u * jnp.tanh(u)


def kernel(
    members, mats, bias, gain, blocks, shifts,
    final_ref, mean_ref,
    w, st_in, st_out, own, halo, spread, recv_term, node_term, hid, fin, acc, acc_in, mean_b,
    w_sem, init_send, st_sem, st_send, halo_sem, halo_send, fin_sem,
    acc_sem, acc_send, mean_sem, mean_send,
):
    sections = lax.axis_size("section")
    units = sections
    s = lax.axis_index("section")
    e = lax.axis_index("ens")
    width = members.shape[-1]
    rows = BLK // CHUNKS
    slots = 6
    last = sections - 1
    pieces = width // LANES

    def chunk(j):
        return pl.ds(j * rows, rows)

    loads = [pltpu.make_async_copy(mats.at[0, i], w.at[i], w_sem.at[i]) for i in range(6)]
    for i in (0, 1, 3, 2, 4, 5):
        loads[i].start()

    barrier = pltpu.get_barrier_semaphore()
    for by in range(1, sections):
        pl.semaphore_signal(barrier, inc=1, device_id={"section": shifted("section", by)}, device_id_type=MESH)
    for by in (1, -1):
        pl.semaphore_signal(barrier, inc=1, device_id={"dom": shifted("dom", by)}, device_id_type=MESH)
    pl.semaphore_signal(barrier, inc=1, device_id={"ens": 1 - e}, device_id_type=MESH)
    pl.semaphore_wait(barrier, sections + 2)

    def init_copy(j):
        return pltpu.make_async_remote_copy(
            members.at[0, chunk(j)], st_in.at[s, chunk(j)], init_send.at[j], st_sem.at[s, j],
            device_id={"section": 0}, device_id_type=MESH)

    def init_local(j):
        return pltpu.make_async_copy(members.at[0, chunk(j)], st_in.at[0, chunk(j)], st_sem.at[0, j])

    def state_copy(m, j):
        return pltpu.make_async_remote_copy(
            st_out.at[m, chunk(j)], st_in.at[m, chunk(j)], st_send.at[m, j], st_sem.at[m, j],
            device_id={"section": lax.rem(s + 1, sections)}, device_id_type=MESH)

    def final_copy(m, j):
        return pltpu.make_async_remote_copy(
            st_out.at[m, chunk(j)], fin.at[chunk(j)], st_send.at[m, j], fin_sem.at[j],
            device_id={"section": m}, device_id_type=MESH)

    def halo_copy(m, side, j):
        return pltpu.make_async_remote_copy(
            own.at[m, chunk(j)], halo.at[m, side, chunk(j)], halo_send.at[m, side, j], halo_sem.at[m, side, j],
            device_id={"dom": shifted("dom", 1 - 2 * side)}, device_id_type=MESH)

    @pl.when(s != 0)
    def _():
        for j in range(CHUNKS):
            init_copy(j).start()

    @pl.when(s == 0)
    def _():
        for j in range(CHUNKS):
            init_local(j).start()

    for i in (0, 1, 3):
        loads[i].wait()
        w[i] = w[i] * jnp.bfloat16(0.5)

    def put_spread(parity, block, j, values):
        values = values.astype(jnp.float32)
        for c in range(pieces):
            part = values[:, c * LANES:(c + 1) * LANES]
            spread[parity, block, c, pl.ds(j * rows, rows), :] = part
            spread[parity, block, c, pl.ds(BLK + j * rows, rows), :] = part

    def enter(m):
        parity = lax.rem(m, 2)
        for j in range(CHUNKS):
            pltpu.make_async_copy(st_in.at[m, chunk(j)], st_in.at[m, chunk(j)], st_sem.at[m, j]).wait()
            terms = mm(st_in[m, chunk(j)], w[0]).astype(jnp.bfloat16)
            own[m, chunk(j)] = terms
            for side in range(2):
                halo_copy(m, side, j).start()
            put_spread(parity, 1, j, terms)
        state = st_in[m]
        recv_term[parity] = mm(state, w[1]) + 0.5 * bias[0, 0:1]
        node_term[parity] = mm(state, w[3]) + 0.5 * bias[0, 1:2]

    def finish(m):
        parity = lax.rem(m, 2)
        for j in range(CHUNKS):
            for side in range(2):
                halo_copy(m, side, j).wait_recv()
                put_spread(parity, 2 * side, j, halo[m, side, chunk(j)])
        for j in range(CHUNKS):
            for k in range(slots):
                block = blocks[0, k]
                start = shifts[0, k] + j * rows
                for c in range(pieces):
                    lanes = slice(c * LANES, (c + 1) * LANES)
                    u = spread[parity, block, c, pl.ds(start, rows), :] + recv_term[parity, chunk(j), lanes]
                    hid[j, pl.ds(k * rows, rows), lanes] = twice_half_silu(u).astype(jnp.bfloat16)
            edge = mm(hid[j], w[2])
            total = None
            for k in range(slots):
                part = edge[k * rows:(k + 1) * rows]
                spread_of = jnp.mean(part * part, axis=-1, keepdims=True)
                part = part * lax.rsqrt(spread_of + EPSILON)
                total = part if total is None else total + part
            messages = (total * gain[0, 0:1]).astype(jnp.bfloat16)
            u = mm(messages, w[4]) + node_term[parity, chunk(j)]
            out = mm(twice_half_silu(u).astype(jnp.bfloat16), w[5])
            spread_of = jnp.mean(out * out, axis=-1, keepdims=True)
            state = st_in[m, chunk(j)].astype(jnp.float32)
            state = (state + out * lax.rsqrt(spread_of + EPSILON) * gain[0, 1:2]).astype(jnp.bfloat16)
            st_out[m, chunk(j)] = state

            @pl.when(s != last)
            def _():
                state_copy(m, j).start()

            @pl.when(s == last)
            def _():
                @pl.when(m != last)
                def _():
                    final_copy(m, j).start()

                @pl.when(m == 0)
                def _():
                    acc[chunk(j)] = st_out[m, chunk(j)].astype(jnp.float32)

                @pl.when(m != 0)
                def _():
                    acc[chunk(j)] = acc[chunk(j)] + st_out[m, chunk(j)].astype(jnp.float32)

    def step(t, carry):
        @pl.when(t < units)
        def _():
            enter(t)

        @pl.when(t == 0)
        def _():
            for i in (2, 5):
                loads[i].wait()
                w[i] = centred(w[i])
            loads[4].wait()
            w[4] = w[4] * jnp.bfloat16(0.5)

        @pl.when(t > 0)
        def _():
            finish(t - 1)

        return carry

    lax.fori_loop(0, units + 1, step, 0)

    half = BLK // 2
    mine = pl.ds(pl.multiple_of(e * half, half), half)
    theirs = pl.ds(pl.multiple_of((1 - e) * half, half), half)

    def mean_out(m, slot):
        return pltpu.make_async_remote_copy(
            mean_b.at[mine], mean_b.at[mine], mean_send.at[slot], mean_sem.at[0],
            device_id={"section": m}, device_id_type=MESH)

    mean_peer = pltpu.make_async_remote_copy(
        mean_b.at[mine], mean_b.at[mine], mean_send.at[sections - 1], mean_sem.at[1],
        device_id={"ens": 1 - e}, device_id_type=MESH)
    acc_peer = pltpu.make_async_remote_copy(
        acc.at[theirs], acc_in, acc_send, acc_sem,
        device_id={"ens": 1 - e}, device_id_type=MESH)
    order = sorted(range(1, sections), key=lambda d: -min(d, sections - d))

    @pl.when(s == last)
    def _():
        acc_peer.start()
        acc_peer.wait()
        mean_b[mine] = ((acc[mine] + acc_in[...]) * (1.0 / (2 * sections))).astype(jnp.bfloat16)
        for slot, d in enumerate(order):
            mean_out(lax.rem(s + d, sections), slot).start()
        mean_peer.start()
        final_ref[0] = st_out[last]
        for slot, d in enumerate(order):
            mean_out(lax.rem(s + d, sections), slot).wait_send()

    @pl.when(s != last)
    def _():
        for j in range(CHUNKS):
            pltpu.make_async_copy(fin.at[chunk(j)], fin.at[chunk(j)], fin_sem.at[j]).wait()
        final_ref[0] = fin[...]
        pltpu.make_async_copy(mean_b.at[mine], mean_b.at[mine], mean_sem.at[0]).wait()
        mean_peer.start()

    mean_peer.wait_send()

    def drain(m, carry):
        for j in range(CHUNKS):
            for side in range(2):
                halo_copy(m, side, j).wait_send()

            @pl.when(s != last)
            def _():
                state_copy(m, j).wait_send()

            @pl.when(jnp.logical_and(s == last, m != last))
            def _():
                final_copy(m, j).wait_send()
        return carry

    lax.fori_loop(0, units, drain, 0)

    @pl.when(s != 0)
    def _():
        for j in range(CHUNKS):
            init_copy(j).wait_send()

    pltpu.make_async_copy(mean_b.at[theirs], mean_b.at[theirs], mean_sem.at[1]).wait()
    mean_ref[...] = mean_b[...].astype(jnp.float32)


def on_device(members, layer_mats, biases, norm_gains, edge_blocks, edge_shift):
    sections = lax.axis_size("section")
    width = members.shape[-1]
    bf16, f32 = jnp.bfloat16, jnp.float32
    dma = pltpu.SemaphoreType.DMA
    vmem = pl.BlockSpec(memory_space=pltpu.VMEM)
    smem = pl.BlockSpec(memory_space=pltpu.SMEM)
    return pl.pallas_call(
        kernel,
        out_shape=(
            jax.ShapeDtypeStruct((1, BLK, width), bf16),
            jax.ShapeDtypeStruct((BLK, width), f32),
        ),
        in_specs=[vmem, pl.BlockSpec(memory_space=pl.ANY), vmem, vmem, smem, smem],
        out_specs=(vmem, vmem),
        scratch_shapes=[
            pltpu.VMEM((6, width, width), bf16),
            pltpu.VMEM((sections, BLK, width), bf16),
            pltpu.VMEM((sections, BLK, width), bf16),
            pltpu.VMEM((sections, BLK, width), bf16),
            pltpu.VMEM((sections, 2, BLK, width), bf16),
            pltpu.VMEM((2, 3, width // LANES, 2 * BLK, LANES), f32),
            pltpu.VMEM((2, BLK, width), f32),
            pltpu.VMEM((2, BLK, width), f32),
            pltpu.VMEM((CHUNKS, 6 * BLK // CHUNKS, width), bf16),
            pltpu.VMEM((BLK, width), bf16),
            pltpu.VMEM((BLK, width), f32),
            pltpu.VMEM((BLK // 2, width), f32),
            pltpu.VMEM((BLK, width), bf16),
            dma((6,)),
            dma((CHUNKS,)),
            dma((sections, CHUNKS)),
            dma((sections, CHUNKS)),
            dma((sections, 2, CHUNKS)),
            dma((sections, 2, CHUNKS)),
            dma((CHUNKS,)),
            dma,
            dma,
            dma((2,)),
            dma((sections,)),
        ],
        compiler_params=pltpu.CompilerParams(
            collective_id=0, has_side_effects=True, vmem_limit_bytes=48 << 20),
    )(members, layer_mats, biases, norm_gains, edge_blocks, edge_shift)


def solution(mesh):
    placed = (
        P(("section", "ens"), "dom", None),
        P("section", None, None, None),
        P("section", None, None),
        P("section", None, None),
        P("dom", None),
        P("dom", None),
    )
    return jax.shard_map(
        on_device,
        mesh=mesh,
        in_specs=placed,
        out_specs=(P(("section", "ens"), "dom", None), P("dom", None)),
        check_vma=False,
    )
```

```python
import jax
import jax.numpy as jnp
from jax import lax
from jax.experimental import pallas as pl
from jax.experimental.pallas import tpu as pltpu
from jax.sharding import PartitionSpec as P

BLK = 128
EPSILON = 1e-05
CHUNKS = 4
LANES = 128
MESH = pl.DeviceIdType.MESH


def shifted(axis, by):
    devices = lax.axis_size(axis)
    return lax.rem(lax.axis_index(axis) + by + devices, devices)


def mm(a, b):
    return jnp.dot(a, b, preferred_element_type=jnp.float32)


def centred(w):
    w = w.astype(jnp.float32)
    return (w - jnp.mean(w, axis=-1, keepdims=True)).astype(jnp.bfloat16)


def twice_half_silu(u):
    return u + u * jnp.tanh(u)


def kernel(
    members, mats, bias_in, gain_in, blocks_in, shifts_in,
    final_ref, mean_ref,
    bias, gain, blocks, shifts, w, st_in, st_out, own, halo, spread, recv_term, node_term, hid, fin, acc, acc_in, mean_b, mean_f,
    small_sem, w_sem, init_send, st_sem, st_send, halo_sem, halo_send, fin_sem,
    acc_sem, acc_send, mean_sem, mean_send, out_sem, go_sem, turn_sem,
):
    sections = lax.axis_size("section")
    units = sections
    s = lax.axis_index("section")
    e = lax.axis_index("ens")
    width = members.shape[-1]
    rows = BLK // CHUNKS
    slots = 6
    last = sections - 1
    pieces = width // LANES

    def chunk(j):
        return pl.ds(j * rows, rows)

    loads = [pltpu.make_async_copy(mats.at[0, i], w.at[i], w_sem.at[i]) for i in range(6)]
    small = [
        pltpu.make_async_copy(a, b, small_sem.at[i])
        for i, (a, b) in enumerate(((blocks_in, blocks), (shifts_in, shifts), (bias_in, bias), (gain_in, gain)))
    ]
    for copy in [loads[0]] + small + [loads[i] for i in (1, 3, 2, 4, 5)]:
        copy.start()

    barrier = pltpu.get_barrier_semaphore()
    for by in range(1, sections):
        pl.semaphore_signal(barrier, inc=1, device_id={"section": shifted("section", by)}, device_id_type=MESH)
    for by in (1, -1):
        pl.semaphore_signal(barrier, inc=1, device_id={"dom": shifted("dom", by)}, device_id_type=MESH)
    pl.semaphore_signal(barrier, inc=1, device_id={"ens": 1 - e}, device_id_type=MESH)
    pl.semaphore_wait(barrier, sections + 2)

    def init_copy(j):
        return pltpu.make_async_remote_copy(
            members.at[0, chunk(j)], st_in.at[s, chunk(j)], init_send.at[j], st_sem.at[s, j],
            device_id={"section": 0}, device_id_type=MESH)

    def init_local(j):
        return pltpu.make_async_copy(members.at[0, chunk(j)], st_in.at[0, chunk(j)], st_sem.at[0, j])

    def state_copy(m, j):
        return pltpu.make_async_remote_copy(
            st_out.at[m, chunk(j)], st_in.at[m, chunk(j)], st_send.at[m, j], st_sem.at[m, j],
            device_id={"section": lax.rem(s + 1, sections)}, device_id_type=MESH)

    def final_copy(m, j):
        return pltpu.make_async_remote_copy(
            st_out.at[m, chunk(j)], fin.at[chunk(j)], st_send.at[m, j], fin_sem.at[j],
            device_id={"section": m}, device_id_type=MESH)

    def halo_copy(m, side, j):
        return pltpu.make_async_remote_copy(
            own.at[m, chunk(j)], halo.at[m, side, chunk(j)], halo_send.at[m, side, j], halo_sem.at[m, side, j],
            device_id={"dom": shifted("dom", 1 - 2 * side)}, device_id_type=MESH)

    relay = sections // 2

    @pl.when(jnp.logical_and(s > 1, s <= relay))
    def _():
        pl.semaphore_wait(go_sem, 1)

    @pl.when(s != 0)
    def _():
        for j in range(CHUNKS):
            init_copy(j).start()

    @pl.when(jnp.logical_and(s > 0, s < relay))
    def _():
        init_copy(0).wait_send()
        pl.semaphore_signal(go_sem, inc=1, device_id={"section": s + 1}, device_id_type=MESH)

    @pl.when(s == 0)
    def _():
        for j in range(CHUNKS):
            init_local(j).start()

    for copy in small:
        copy.wait()
    for i in (0, 1, 3):
        loads[i].wait()
        w[i] = w[i] * jnp.bfloat16(0.5)

    def put_spread(parity, block, j, values):
        values = values.astype(jnp.float32)
        for c in range(pieces):
            part = values[:, c * LANES:(c + 1) * LANES]
            spread[parity, block, c, pl.ds(j * rows, rows), :] = part
            spread[parity, block, c, pl.ds(BLK + j * rows, rows), :] = part

    def enter(m):
        parity = lax.rem(m, 2)
        for j in range(CHUNKS):
            pltpu.make_async_copy(st_in.at[m, chunk(j)], st_in.at[m, chunk(j)], st_sem.at[m, j]).wait()
            terms = mm(st_in[m, chunk(j)], w[0]).astype(jnp.bfloat16)
            own[m, chunk(j)] = terms
            for side in range(2):
                halo_copy(m, side, j).start()
            put_spread(parity, 1, j, terms)
        state = st_in[m]
        recv_term[parity] = mm(state, w[1]) + 0.5 * bias[0, 0:1]
        node_term[parity] = mm(state, w[3]) + 0.5 * bias[0, 1:2]

    def finish(m):
        parity = lax.rem(m, 2)
        for j in range(CHUNKS):
            for side in range(2):
                halo_copy(m, side, j).wait_recv()
                put_spread(parity, 2 * side, j, halo[m, side, chunk(j)])
        for k in range(slots):
            block = blocks[0, k]
            for c in range(pieces):
                lanes = slice(c * LANES, (c + 1) * LANES)
                u = spread[parity, block, c, pl.ds(shifts[0, k], BLK), :] + recv_term[parity, :, lanes]
                hid[pl.ds(k * BLK, BLK), lanes] = twice_half_silu(u).astype(jnp.bfloat16)
        edge = mm(hid[...], w[2])
        total = None
        for k in range(slots):
            part = edge[k * BLK:(k + 1) * BLK]
            spread_of = jnp.mean(part * part, axis=-1, keepdims=True)
            part = part * lax.rsqrt(spread_of + EPSILON)
            total = part if total is None else total + part
        messages = (total * gain[0, 0:1]).astype(jnp.bfloat16)
        u = mm(messages, w[4]) + node_term[parity]
        out = mm(twice_half_silu(u).astype(jnp.bfloat16), w[5])
        spread_of = jnp.mean(out * out, axis=-1, keepdims=True)
        state = st_in[m].astype(jnp.float32)
        state = (state + out * lax.rsqrt(spread_of + EPSILON) * gain[0, 1:2]).astype(jnp.bfloat16)
        st_out[m] = state

        for j in range(CHUNKS):
            @pl.when(s != last)
            def _():
                state_copy(m, j).start()

            @pl.when(s == last)
            def _():
                @pl.when(m != last)
                def _():
                    final_copy(m, j).start()

                @pl.when(m == 0)
                def _():
                    acc[chunk(j)] = st_out[m, chunk(j)].astype(jnp.float32)

                @pl.when(m != 0)
                def _():
                    acc[chunk(j)] = acc[chunk(j)] + st_out[m, chunk(j)].astype(jnp.float32)

    @pl.when(jnp.logical_and(s == 0, e == 1))
    def _():
        pl.semaphore_wait(turn_sem, 1)

    def step(t, carry):
        @pl.when(t < units)
        def _():
            enter(t)

        @pl.when(t == 0)
        def _():
            for i in (2, 5):
                loads[i].wait()
                w[i] = centred(w[i])
            loads[4].wait()
            w[4] = w[4] * jnp.bfloat16(0.5)

            @pl.when(jnp.logical_and(s == 0, e == 0))
            def _():
                pl.semaphore_signal(turn_sem, inc=1, device_id={"ens": 1 - e}, device_id_type=MESH)

        @pl.when(t > 0)
        def _():
            finish(t - 1)

        return carry

    lax.fori_loop(0, units + 1, step, 0)

    half = BLK // 2
    mine = pl.ds(pl.multiple_of(e * half, half), half)
    theirs = pl.ds(pl.multiple_of((1 - e) * half, half), half)

    def mean_out(m, slot):
        return pltpu.make_async_remote_copy(
            mean_b.at[mine], mean_b.at[mine], mean_send.at[slot], mean_sem.at[0],
            device_id={"section": m}, device_id_type=MESH)

    mean_peer = pltpu.make_async_remote_copy(
        mean_b.at[mine], mean_b.at[mine], mean_send.at[sections - 1], mean_sem.at[1],
        device_id={"ens": 1 - e}, device_id_type=MESH)
    acc_peer = pltpu.make_async_remote_copy(
        acc.at[theirs], acc_in, acc_send, acc_sem,
        device_id={"ens": 1 - e}, device_id_type=MESH)
    order = sorted(range(1, sections), key=lambda d: -min(d, sections - d))

    @pl.when(s == last)
    def _():
        acc_peer.start()
        acc_peer.wait()
        mean_b[mine] = ((acc[mine] + acc_in[...]) * (1.0 / (2 * sections))).astype(jnp.bfloat16)
        for slot, d in enumerate(order):
            mean_out(lax.rem(s + d, sections), slot).start()
        mean_peer.start()
        pltpu.make_async_copy(st_out.at[last], final_ref.at[0], out_sem.at[0]).start()
        for slot, d in enumerate(order):
            mean_out(lax.rem(s + d, sections), slot).wait_send()

    @pl.when(s != last)
    def _():
        for j in range(CHUNKS):
            pltpu.make_async_copy(fin.at[chunk(j)], fin.at[chunk(j)], fin_sem.at[j]).wait()
        pltpu.make_async_copy(fin, final_ref.at[0], out_sem.at[0]).start()
        pltpu.make_async_copy(mean_b.at[mine], mean_b.at[mine], mean_sem.at[0]).wait()
        mean_peer.start()

    mean_peer.wait_send()

    def drain(m, carry):
        for j in range(CHUNKS):
            for side in range(2):
                halo_copy(m, side, j).wait_send()

            @pl.when(s != last)
            def _():
                state_copy(m, j).wait_send()

            @pl.when(jnp.logical_and(s == last, m != last))
            def _():
                final_copy(m, j).wait_send()
        return carry

    lax.fori_loop(0, units, drain, 0)

    @pl.when(s != 0)
    def _():
        for j in range(1, CHUNKS):
            init_copy(j).wait_send()

    @pl.when(s >= relay)
    def _():
        init_copy(0).wait_send()

    pltpu.make_async_copy(mean_b.at[theirs], mean_b.at[theirs], mean_sem.at[1]).wait()
    mean_f[...] = mean_b[...].astype(jnp.float32)
    mean_done = pltpu.make_async_copy(mean_f, mean_ref, out_sem.at[1])
    mean_done.start()
    pltpu.make_async_copy(fin, final_ref.at[0], out_sem.at[0]).wait()
    mean_done.wait()


def on_device(members, layer_mats, biases, norm_gains, edge_blocks, edge_shift):
    sections = lax.axis_size("section")
    width = members.shape[-1]
    bf16, f32 = jnp.bfloat16, jnp.float32
    dma = pltpu.SemaphoreType.DMA
    anywhere = pl.BlockSpec(memory_space=pl.ANY)
    return pl.pallas_call(
        kernel,
        out_shape=(
            jax.ShapeDtypeStruct((1, BLK, width), bf16),
            jax.ShapeDtypeStruct((BLK, width), f32),
        ),
        in_specs=[anywhere] * 6,
        out_specs=(anywhere, anywhere),
        scratch_shapes=[
            pltpu.VMEM((1, 2, width), f32),
            pltpu.VMEM((1, 2, width), f32),
            pltpu.SMEM((1, 6), jnp.int32),
            pltpu.SMEM((1, 6), jnp.int32),
            pltpu.VMEM((6, width, width), bf16),
            pltpu.VMEM((sections, BLK, width), bf16),
            pltpu.VMEM((sections, BLK, width), bf16),
            pltpu.VMEM((sections, BLK, width), bf16),
            pltpu.VMEM((sections, 2, BLK, width), bf16),
            pltpu.VMEM((2, 3, width // LANES, 2 * BLK, LANES), f32),
            pltpu.VMEM((2, BLK, width), f32),
            pltpu.VMEM((2, BLK, width), f32),
            pltpu.VMEM((6 * BLK, width), bf16),
            pltpu.VMEM((BLK, width), bf16),
            pltpu.VMEM((BLK, width), f32),
            pltpu.VMEM((BLK // 2, width), f32),
            pltpu.VMEM((BLK, width), bf16),
            pltpu.VMEM((BLK, width), f32),
            dma((4,)),
            dma((6,)),
            dma((CHUNKS,)),
            dma((sections, CHUNKS)),
            dma((sections, CHUNKS)),
            dma((sections, 2, CHUNKS)),
            dma((sections, 2, CHUNKS)),
            dma((CHUNKS,)),
            dma,
            dma,
            dma((2,)),
            dma((sections,)),
            dma((2,)),
            pltpu.SemaphoreType.REGULAR,
            pltpu.SemaphoreType.REGULAR,
        ],
        compiler_params=pltpu.CompilerParams(
            collective_id=0, has_side_effects=True, vmem_limit_bytes=60 << 20),
    )(members, layer_mats, biases, norm_gains, edge_blocks, edge_shift)


def solution(mesh):
    placed = (
        P(("section", "ens"), "dom", None),
        P("section", None, None, None),
        P("section", None, None),
        P("section", None, None),
        P("dom", None),
        P("dom", None),
    )
    return jax.shard_map(
        on_device,
        mesh=mesh,
        in_specs=placed,
        out_specs=(P(("section", "ens"), "dom", None), P("dom", None)),
        check_vma=False,
    )
```

```python
import jax
import jax.numpy as jnp
from jax import lax
from jax.experimental import pallas as pl
from jax.experimental.pallas import tpu as pltpu
from jax.sharding import PartitionSpec as P

BLK = 128
EPSILON = 1e-05
CHUNKS = 4
LANES = 128
MESH = pl.DeviceIdType.MESH


def shifted(axis, by):
    devices = lax.axis_size(axis)
    return lax.rem(lax.axis_index(axis) + by + devices, devices)


def mm(a, b):
    return jnp.dot(a, b, preferred_element_type=jnp.float32)


def centred(w):
    w = w.astype(jnp.float32)
    return (w - jnp.mean(w, axis=-1, keepdims=True)).astype(jnp.bfloat16)


def twice_half_silu(u):
    return u + u * jnp.tanh(u)


def kernel(
    members, mats, bias_in, gain_in, blocks_in, shifts_in,
    final_ref, mean_ref,
    bias, gain, blocks, shifts, w, st_in, st_out, own, halo, spread, recv_term, node_term, hid, fin, acc, acc_in, mean_b, mean_f,
    small_sem, w_sem, init_send, st_sem, st_send, halo_sem, halo_send, fin_sem,
    acc_sem, acc_send, mean_sem, mean_send, out_sem, go_sem, turn_sem,
):
    sections = lax.axis_size("section")
    units = sections
    s = lax.axis_index("section")
    e = lax.axis_index("ens")
    width = members.shape[-1]
    rows = BLK // CHUNKS
    slots = 6
    last = sections - 1
    pieces = width // LANES

    d = lax.axis_index("dom")
    after = (lax.rem(s + 1, sections), d, e)
    beside = [(s, shifted("dom", by), e) for by in (1, -1)]

    def chunk(j):
        return pl.ds(j * rows, rows)

    loads = [pltpu.make_async_copy(mats.at[0, i], w.at[i], w_sem.at[i]) for i in range(6)]
    small = [
        pltpu.make_async_copy(a, b, small_sem.at[i])
        for i, (a, b) in enumerate(((blocks_in, blocks), (shifts_in, shifts), (bias_in, bias), (gain_in, gain)))
    ]
    for copy in [loads[0]] + small + [loads[i] for i in (1, 3, 2, 4, 5)]:
        copy.start()

    barrier = pltpu.get_barrier_semaphore()
    for by in range(1, sections):
        pl.semaphore_signal(barrier, inc=1, device_id={"section": shifted("section", by)}, device_id_type=MESH)
    for by in (1, -1):
        pl.semaphore_signal(barrier, inc=1, device_id={"dom": shifted("dom", by)}, device_id_type=MESH)
    pl.semaphore_signal(barrier, inc=1, device_id={"ens": 1 - e}, device_id_type=MESH)
    pl.semaphore_wait(barrier, sections + 2)

    def init_copy(j):
        return pltpu.make_async_remote_copy(
            members.at[0, chunk(j)], st_in.at[s, chunk(j)], init_send.at[j], st_sem.at[s, j],
            device_id={"section": 0}, device_id_type=MESH)

    def init_local(j):
        return pltpu.make_async_copy(members.at[0, chunk(j)], st_in.at[0, chunk(j)], st_sem.at[0, j])

    def state_copy(m, j):
        return pltpu.make_async_remote_copy(
            st_out.at[m, chunk(j)], st_in.at[m, chunk(j)], st_send.at[m, j], st_sem.at[m, j],
            device_id=after, device_id_type=MESH)

    def final_copy(m, j):
        return pltpu.make_async_remote_copy(
            st_out.at[m, chunk(j)], fin.at[chunk(j)], st_send.at[m, j], fin_sem.at[j],
            device_id=(m, d, e), device_id_type=MESH)

    def halo_copy(m, side, j):
        return pltpu.make_async_remote_copy(
            own.at[m, chunk(j)], halo.at[m, side, chunk(j)], halo_send.at[m], halo_sem.at[m],
            device_id=beside[side], device_id_type=MESH)

    relay = sections // 2

    @pl.when(jnp.logical_and(s > 1, s <= relay))
    def _():
        pl.semaphore_wait(go_sem, 1)

    @pl.when(s != 0)
    def _():
        for j in range(CHUNKS):
            init_copy(j).start()

    @pl.when(jnp.logical_and(s > 0, s < relay))
    def _():
        init_copy(0).wait_send()
        pl.semaphore_signal(go_sem, inc=1, device_id={"section": s + 1}, device_id_type=MESH)

    @pl.when(s == 0)
    def _():
        for j in range(CHUNKS):
            init_local(j).start()

    for copy in small:
        copy.wait()
    for i in (0, 1, 3):
        loads[i].wait()
        w[i] = w[i] * jnp.bfloat16(0.5)

    def put_spread(parity, block, j, values):
        values = values.astype(jnp.float32)
        for c in range(pieces):
            part = values[:, c * LANES:(c + 1) * LANES]
            spread[parity, block, c, pl.ds(j * rows, rows), :] = part
            spread[parity, block, c, pl.ds(BLK + j * rows, rows), :] = part

    def enter(m):
        parity = lax.rem(m, 2)
        for j in range(CHUNKS):
            pltpu.make_async_copy(st_in.at[m, chunk(j)], st_in.at[m, chunk(j)], st_sem.at[m, j]).wait()
            terms = mm(st_in[m, chunk(j)], w[0]).astype(jnp.bfloat16)
            own[m, chunk(j)] = terms
            for side in range(2):
                halo_copy(m, side, j).start()
            put_spread(parity, 1, j, terms)
        state = st_in[m]
        recv_term[parity] = mm(state, w[1]) + 0.5 * bias[0, 0:1]
        node_term[parity] = mm(state, w[3]) + 0.5 * bias[0, 1:2]

    def finish(m):
        parity = lax.rem(m, 2)
        pltpu.make_async_copy(halo.at[m], halo.at[m], halo_sem.at[m]).wait()
        for j in range(CHUNKS):
            for side in range(2):
                put_spread(parity, 2 * side, j, halo[m, side, chunk(j)])
        for k in range(slots):
            block = blocks[0, k]
            for c in range(pieces):
                lanes = slice(c * LANES, (c + 1) * LANES)
                u = spread[parity, block, c, pl.ds(shifts[0, k], BLK), :] + recv_term[parity, :, lanes]
                hid[pl.ds(k * BLK, BLK), lanes] = twice_half_silu(u).astype(jnp.bfloat16)
        edge = mm(hid[...], w[2])
        total = None
        for k in range(slots):
            part = edge[k * BLK:(k + 1) * BLK]
            spread_of = jnp.mean(part * part, axis=-1, keepdims=True)
            part = part * lax.rsqrt(spread_of + EPSILON)
            total = part if total is None else total + part
        messages = (total * gain[0, 0:1]).astype(jnp.bfloat16)
        u = mm(messages, w[4]) + node_term[parity]
        out = mm(twice_half_silu(u).astype(jnp.bfloat16), w[5])
        spread_of = jnp.mean(out * out, axis=-1, keepdims=True)
        state = st_in[m].astype(jnp.float32)
        state = (state + out * lax.rsqrt(spread_of + EPSILON) * gain[0, 1:2]).astype(jnp.bfloat16)
        st_out[m] = state

        @pl.when(s != last)
        def _():
            for j in range(CHUNKS):
                state_copy(m, j).start()

        @pl.when(s == last)
        def _():
            @pl.when(m != last)
            def _():
                for j in range(CHUNKS):
                    final_copy(m, j).start()

            @pl.when(m == 0)
            def _():
                acc[...] = st_out[m].astype(jnp.float32)

            @pl.when(m != 0)
            def _():
                acc[...] = acc[...] + st_out[m].astype(jnp.float32)

    @pl.when(jnp.logical_and(s == 0, e == 1))
    def _():
        pl.semaphore_wait(turn_sem, 1)

    def step(t, carry):
        @pl.when(t < units)
        def _():
            enter(t)

        @pl.when(t == 0)
        def _():
            for i in (2, 5):
                loads[i].wait()
                w[i] = centred(w[i])
            loads[4].wait()
            w[4] = w[4] * jnp.bfloat16(0.5)

            @pl.when(jnp.logical_and(s == 0, e == 0))
            def _():
                pl.semaphore_signal(turn_sem, inc=1, device_id={"ens": 1 - e}, device_id_type=MESH)

        @pl.when(t > 0)
        def _():
            finish(t - 1)

        return carry

    lax.fori_loop(0, units + 1, step, 0)

    half = BLK // 2
    mine = pl.ds(pl.multiple_of(e * half, half), half)
    theirs = pl.ds(pl.multiple_of((1 - e) * half, half), half)

    def mean_out(m, slot):
        return pltpu.make_async_remote_copy(
            mean_b.at[mine], mean_b.at[mine], mean_send.at[slot], mean_sem.at[0],
            device_id={"section": m}, device_id_type=MESH)

    mean_peer = pltpu.make_async_remote_copy(
        mean_b.at[mine], mean_b.at[mine], mean_send.at[sections - 1], mean_sem.at[1],
        device_id={"ens": 1 - e}, device_id_type=MESH)
    acc_peer = pltpu.make_async_remote_copy(
        acc.at[theirs], acc_in, acc_send, acc_sem,
        device_id={"ens": 1 - e}, device_id_type=MESH)
    order = sorted(range(1, sections), key=lambda d: -min(d, sections - d))

    @pl.when(s == last)
    def _():
        acc_peer.start()
        acc_peer.wait()
        mean_b[mine] = ((acc[mine] + acc_in[...]) * (1.0 / (2 * sections))).astype(jnp.bfloat16)
        for slot, d in enumerate(order):
            mean_out(lax.rem(s + d, sections), slot).start()
        mean_peer.start()
        pltpu.make_async_copy(st_out.at[last], final_ref.at[0], out_sem.at[0]).start()
        for slot, d in enumerate(order):
            mean_out(lax.rem(s + d, sections), slot).wait_send()

    @pl.when(s != last)
    def _():
        for j in range(CHUNKS):
            pltpu.make_async_copy(fin.at[chunk(j)], fin.at[chunk(j)], fin_sem.at[j]).wait()
        pltpu.make_async_copy(fin, final_ref.at[0], out_sem.at[0]).start()
        pltpu.make_async_copy(mean_b.at[mine], mean_b.at[mine], mean_sem.at[0]).wait()
        mean_peer.start()

    mean_peer.wait_send()

    def drain(m, carry):
        pltpu.make_async_copy(halo.at[m], halo.at[m], halo_send.at[m]).wait()
        for j in range(CHUNKS):
            @pl.when(s != last)
            def _():
                state_copy(m, j).wait_send()

            @pl.when(jnp.logical_and(s == last, m != last))
            def _():
                final_copy(m, j).wait_send()
        return carry

    lax.fori_loop(0, units, drain, 0)

    @pl.when(s != 0)
    def _():
        for j in range(1, CHUNKS):
            init_copy(j).wait_send()

    @pl.when(s >= relay)
    def _():
        init_copy(0).wait_send()

    pltpu.make_async_copy(mean_b.at[theirs], mean_b.at[theirs], mean_sem.at[1]).wait()
    mean_f[...] = mean_b[...].astype(jnp.float32)
    mean_done = pltpu.make_async_copy(mean_f, mean_ref, out_sem.at[1])
    mean_done.start()
    pltpu.make_async_copy(fin, final_ref.at[0], out_sem.at[0]).wait()
    mean_done.wait()


def on_device(members, layer_mats, biases, norm_gains, edge_blocks, edge_shift):
    sections = lax.axis_size("section")
    width = members.shape[-1]
    bf16, f32 = jnp.bfloat16, jnp.float32
    dma = pltpu.SemaphoreType.DMA
    anywhere = pl.BlockSpec(memory_space=pl.ANY)
    return pl.pallas_call(
        kernel,
        out_shape=(
            jax.ShapeDtypeStruct((1, BLK, width), bf16),
            jax.ShapeDtypeStruct((BLK, width), f32),
        ),
        in_specs=[anywhere] * 6,
        out_specs=(anywhere, anywhere),
        scratch_shapes=[
            pltpu.VMEM((1, 2, width), f32),
            pltpu.VMEM((1, 2, width), f32),
            pltpu.SMEM((1, 6), jnp.int32),
            pltpu.SMEM((1, 6), jnp.int32),
            pltpu.VMEM((6, width, width), bf16),
            pltpu.VMEM((sections, BLK, width), bf16),
            pltpu.VMEM((sections, BLK, width), bf16),
            pltpu.VMEM((sections, BLK, width), bf16),
            pltpu.VMEM((sections, 2, BLK, width), bf16),
            pltpu.VMEM((2, 3, width // LANES, 2 * BLK, LANES), f32),
            pltpu.VMEM((2, BLK, width), f32),
            pltpu.VMEM((2, BLK, width), f32),
            pltpu.VMEM((6 * BLK, width), bf16),
            pltpu.VMEM((BLK, width), bf16),
            pltpu.VMEM((BLK, width), f32),
            pltpu.VMEM((BLK // 2, width), f32),
            pltpu.VMEM((BLK, width), bf16),
            pltpu.VMEM((BLK, width), f32),
            dma((4,)),
            dma((6,)),
            dma((CHUNKS,)),
            dma((sections, CHUNKS)),
            dma((sections, CHUNKS)),
            dma((sections,)),
            dma((sections,)),
            dma((CHUNKS,)),
            dma,
            dma,
            dma((2,)),
            dma((sections,)),
            dma((2,)),
            pltpu.SemaphoreType.REGULAR,
            pltpu.SemaphoreType.REGULAR,
        ],
        compiler_params=pltpu.CompilerParams(
            collective_id=0, has_side_effects=True, vmem_limit_bytes=60 << 20),
    )(members, layer_mats, biases, norm_gains, edge_blocks, edge_shift)


def solution(mesh):
    placed = (
        P(("section", "ens"), "dom", None),
        P("section", None, None, None),
        P("section", None, None),
        P("section", None, None),
        P("dom", None),
        P("dom", None),
    )
    return jax.shard_map(
        on_device,
        mesh=mesh,
        in_specs=placed,
        out_specs=(P(("section", "ens"), "dom", None), P("dom", None)),
        check_vma=False,
    )
```

```python
import jax
import jax.numpy as jnp
from jax import lax
from jax.experimental import pallas as pl
from jax.experimental.pallas import tpu as pltpu
from jax.sharding import PartitionSpec as P

BLK = 128
EPSILON = 1e-05
CHUNKS = 4
LANES = 128
MESH = pl.DeviceIdType.MESH


def shifted(axis, by):
    devices = lax.axis_size(axis)
    return lax.rem(lax.axis_index(axis) + by + devices, devices)


def mm(a, b):
    return jnp.dot(a, b, preferred_element_type=jnp.float32)


def centred(w):
    w = w.astype(jnp.float32)
    return (w - jnp.mean(w, axis=-1, keepdims=True)).astype(jnp.bfloat16)


def twice_half_silu(u):
    return u + u * jnp.tanh(u)


def kernel(
    members, mats, bias_in, gain_in, blocks_in, shifts_in,
    final_ref, mean_ref,
    bias, gain, blocks, shifts, w, st_in, st_out, own, halo, spread, recv_term, node_term, hid, fin, acc, acc_in, mean_b,
    small_sem, w_sem, init_send, st_sem, st_send, halo_sem, halo_send, fin_sem,
    acc_sem, acc_send, mean_sem, mean_send, out_sem, go_sem, turn_sem,
):
    sections = lax.axis_size("section")
    units = sections
    s = lax.axis_index("section")
    e = lax.axis_index("ens")
    width = members.shape[-1]
    rows = BLK // CHUNKS
    slots = 6
    last = sections - 1
    pieces = width // LANES

    d = lax.axis_index("dom")
    after = (lax.rem(s + 1, sections), d, e)
    beside = [(s, shifted("dom", by), e) for by in (1, -1)]

    def chunk(j):
        return pl.ds(j * rows, rows)

    loads = [pltpu.make_async_copy(mats.at[0, i], w.at[i], w_sem.at[i]) for i in range(6)]
    small = [
        pltpu.make_async_copy(a, b, small_sem.at[i])
        for i, (a, b) in enumerate(((blocks_in, blocks), (shifts_in, shifts), (bias_in, bias), (gain_in, gain)))
    ]
    for copy in [loads[0]] + small + [loads[i] for i in (1, 3, 2, 4, 5)]:
        copy.start()

    barrier = pltpu.get_barrier_semaphore()
    for by in range(1, sections):
        pl.semaphore_signal(barrier, inc=1, device_id={"section": shifted("section", by)}, device_id_type=MESH)
    for by in (1, -1):
        pl.semaphore_signal(barrier, inc=1, device_id={"dom": shifted("dom", by)}, device_id_type=MESH)
    pl.semaphore_signal(barrier, inc=1, device_id={"ens": 1 - e}, device_id_type=MESH)
    for copy in small:
        copy.wait()
    for i in (0, 1, 3):
        loads[i].wait()
        w[i] = w[i] * jnp.bfloat16(0.5)
    pl.semaphore_wait(barrier, sections + 2)

    def init_copy(j):
        return pltpu.make_async_remote_copy(
            members.at[0, chunk(j)], st_in.at[s, chunk(j)], init_send.at[j], st_sem.at[s, j],
            device_id={"section": 0}, device_id_type=MESH)

    def init_local(j):
        return pltpu.make_async_copy(members.at[0, chunk(j)], st_in.at[0, chunk(j)], st_sem.at[0, j])

    def state_copy(m, j):
        return pltpu.make_async_remote_copy(
            st_out.at[m, chunk(j)], st_in.at[m, chunk(j)], st_send.at[m, j], st_sem.at[m, j],
            device_id=after, device_id_type=MESH)

    def final_copy(m, j):
        return pltpu.make_async_remote_copy(
            st_out.at[m, chunk(j)], fin.at[chunk(j)], st_send.at[m, j], fin_sem.at[j],
            device_id=(m, d, e), device_id_type=MESH)

    def halo_copy(m, side, j):
        return pltpu.make_async_remote_copy(
            own.at[m, chunk(j)], halo.at[m, side, chunk(j)], halo_send.at[m], halo_sem.at[m],
            device_id=beside[side], device_id_type=MESH)

    relay = sections // 2

    @pl.when(jnp.logical_and(s > 1, s <= relay))
    def _():
        pl.semaphore_wait(go_sem, 1)

    @pl.when(s != 0)
    def _():
        for j in range(CHUNKS):
            init_copy(j).start()

    @pl.when(jnp.logical_and(s > 0, s < relay))
    def _():
        init_copy(0).wait_send()
        pl.semaphore_signal(go_sem, inc=1, device_id={"section": s + 1}, device_id_type=MESH)

    @pl.when(s == 0)
    def _():
        for j in range(CHUNKS):
            init_local(j).start()


    def put_spread(parity, block, j, values):
        values = values.astype(jnp.float32)
        for c in range(pieces):
            part = values[:, c * LANES:(c + 1) * LANES]
            spread[parity, block, c, pl.ds(j * rows, rows), :] = part
            spread[parity, block, c, pl.ds(BLK + j * rows, rows), :] = part

    def enter(m):
        parity = lax.rem(m, 2)
        for j in range(CHUNKS):
            pltpu.make_async_copy(st_in.at[m, chunk(j)], st_in.at[m, chunk(j)], st_sem.at[m, j]).wait()
            terms = mm(st_in[m, chunk(j)], w[0]).astype(jnp.bfloat16)
            own[m, chunk(j)] = terms
            for side in range(2):
                halo_copy(m, side, j).start()
            put_spread(parity, 1, j, terms)
        state = st_in[m]
        recv_term[parity] = mm(state, w[1]) + 0.5 * bias[0, 0:1]
        node_term[parity] = mm(state, w[3]) + 0.5 * bias[0, 1:2]

    def finish(m):
        parity = lax.rem(m, 2)
        pltpu.make_async_copy(halo.at[m], halo.at[m], halo_sem.at[m]).wait()
        for j in range(CHUNKS):
            for side in range(2):
                put_spread(parity, 2 * side, j, halo[m, side, chunk(j)])
        for k in range(slots):
            block = blocks[0, k]
            for c in range(pieces):
                lanes = slice(c * LANES, (c + 1) * LANES)
                u = spread[parity, block, c, pl.ds(shifts[0, k], BLK), :] + recv_term[parity, :, lanes]
                hid[pl.ds(k * BLK, BLK), lanes] = twice_half_silu(u).astype(jnp.bfloat16)
        edge = mm(hid[...], w[2])
        total = None
        for k in range(slots):
            part = edge[k * BLK:(k + 1) * BLK]
            spread_of = jnp.mean(part * part, axis=-1, keepdims=True)
            part = part * lax.rsqrt(spread_of + EPSILON)
            total = part if total is None else total + part
        messages = (total * gain[0, 0:1]).astype(jnp.bfloat16)
        u = mm(messages, w[4]) + node_term[parity]
        out = mm(twice_half_silu(u).astype(jnp.bfloat16), w[5])
        spread_of = jnp.mean(out * out, axis=-1, keepdims=True)
        state = st_in[m].astype(jnp.float32)
        state = (state + out * lax.rsqrt(spread_of + EPSILON) * gain[0, 1:2]).astype(jnp.bfloat16)
        st_out[m] = state

        @pl.when(s != last)
        def _():
            for j in range(CHUNKS):
                state_copy(m, j).start()

        @pl.when(s == last)
        def _():
            @pl.when(m != last)
            def _():
                for j in range(CHUNKS):
                    final_copy(m, j).start()

            @pl.when(m == 0)
            def _():
                acc[...] = st_out[m].astype(jnp.float32)

            @pl.when(m != 0)
            def _():
                acc[...] = acc[...] + st_out[m].astype(jnp.float32)

    @pl.when(jnp.logical_and(s == 0, e == 1))
    def _():
        pl.semaphore_wait(turn_sem, 1)

    def step(t, carry):
        @pl.when(t < units)
        def _():
            enter(t)

        @pl.when(t == 0)
        def _():
            for i in (2, 5):
                loads[i].wait()
                w[i] = centred(w[i])
            loads[4].wait()
            w[4] = w[4] * jnp.bfloat16(0.5)

            @pl.when(jnp.logical_and(s == 0, e == 0))
            def _():
                pl.semaphore_signal(turn_sem, inc=1, device_id={"ens": 1 - e}, device_id_type=MESH)

        @pl.when(t > 0)
        def _():
            finish(t - 1)

        return carry

    lax.fori_loop(0, units + 1, step, 0)

    half = BLK // 2
    mine = pl.ds(pl.multiple_of(e * half, half), half)
    theirs = pl.ds(pl.multiple_of((1 - e) * half, half), half)

    def mean_out(m, slot):
        return pltpu.make_async_remote_copy(
            mean_b.at[mine], mean_b.at[mine], mean_send.at[slot], mean_sem.at[0],
            device_id={"section": m}, device_id_type=MESH)

    mean_peer = pltpu.make_async_remote_copy(
        mean_b.at[mine], mean_b.at[mine], mean_send.at[sections - 1], mean_sem.at[1],
        device_id={"ens": 1 - e}, device_id_type=MESH)
    acc_peer = pltpu.make_async_remote_copy(
        acc.at[theirs], acc_in, acc_send, acc_sem,
        device_id={"ens": 1 - e}, device_id_type=MESH)
    order = sorted(range(1, sections), key=lambda d: -min(d, sections - d))

    @pl.when(s == last)
    def _():
        acc_peer.start()
        acc_peer.wait()
        mean_b[mine] = ((acc[mine] + acc_in[...]) * (1.0 / (2 * sections))).astype(jnp.bfloat16)
        for slot, d in enumerate(order):
            mean_out(lax.rem(s + d, sections), slot).start()
        mean_peer.start()
        pltpu.make_async_copy(st_out.at[last], final_ref.at[0], out_sem.at[0]).start()

    def drain(m, carry):
        pltpu.make_async_copy(halo.at[m], halo.at[m], halo_send.at[m]).wait()
        for j in range(CHUNKS):
            @pl.when(s != last)
            def _():
                state_copy(m, j).wait_send()

            @pl.when(jnp.logical_and(s == last, m != last))
            def _():
                final_copy(m, j).wait_send()
        return carry

    lax.fori_loop(0, units, drain, 0)

    @pl.when(s != 0)
    def _():
        for j in range(1, CHUNKS):
            init_copy(j).wait_send()

    @pl.when(s >= relay)
    def _():
        init_copy(0).wait_send()

    @pl.when(s == last)
    def _():
        for slot, d in enumerate(order):
            mean_out(lax.rem(s + d, sections), slot).wait_send()

    @pl.when(s != last)
    def _():
        for j in range(CHUNKS):
            pltpu.make_async_copy(fin.at[chunk(j)], fin.at[chunk(j)], fin_sem.at[j]).wait()
        pltpu.make_async_copy(fin, final_ref.at[0], out_sem.at[0]).start()
        pltpu.make_async_copy(mean_b.at[mine], mean_b.at[mine], mean_sem.at[0]).wait()
        mean_peer.start()

    pltpu.make_async_copy(mean_b.at[theirs], mean_b.at[theirs], mean_sem.at[1]).wait()
    mean_done = pltpu.make_async_copy(mean_b, mean_ref, out_sem.at[1])
    mean_done.start()
    mean_peer.wait_send()
    pltpu.make_async_copy(fin, final_ref.at[0], out_sem.at[0]).wait()
    mean_done.wait()


def on_device(members, layer_mats, biases, norm_gains, edge_blocks, edge_shift):
    sections = lax.axis_size("section")
    width = members.shape[-1]
    bf16, f32 = jnp.bfloat16, jnp.float32
    dma = pltpu.SemaphoreType.DMA
    anywhere = pl.BlockSpec(memory_space=pl.ANY)
    final_state, mean = pl.pallas_call(
        kernel,
        out_shape=(
            jax.ShapeDtypeStruct((1, BLK, width), bf16),
            jax.ShapeDtypeStruct((BLK, width), bf16),
        ),
        in_specs=[anywhere] * 6,
        out_specs=(anywhere, anywhere),
        scratch_shapes=[
            pltpu.VMEM((1, 2, width), f32),
            pltpu.VMEM((1, 2, width), f32),
            pltpu.SMEM((1, 6), jnp.int32),
            pltpu.SMEM((1, 6), jnp.int32),
            pltpu.VMEM((6, width, width), bf16),
            pltpu.VMEM((sections, BLK, width), bf16),
            pltpu.VMEM((sections, BLK, width), bf16),
            pltpu.VMEM((sections, BLK, width), bf16),
            pltpu.VMEM((sections, 2, BLK, width), bf16),
            pltpu.VMEM((2, 3, width // LANES, 2 * BLK, LANES), f32),
            pltpu.VMEM((2, BLK, width), f32),
            pltpu.VMEM((2, BLK, width), f32),
            pltpu.VMEM((6 * BLK, width), bf16),
            pltpu.VMEM((BLK, width), bf16),
            pltpu.VMEM((BLK, width), f32),
            pltpu.VMEM((BLK // 2, width), f32),
            pltpu.VMEM((BLK, width), bf16),
            dma((4,)),
            dma((6,)),
            dma((CHUNKS,)),
            dma((sections, CHUNKS)),
            dma((sections, CHUNKS)),
            dma((sections,)),
            dma((sections,)),
            dma((CHUNKS,)),
            dma,
            dma,
            dma((2,)),
            dma((sections,)),
            dma((2,)),
            pltpu.SemaphoreType.REGULAR,
            pltpu.SemaphoreType.REGULAR,
        ],
        compiler_params=pltpu.CompilerParams(
            collective_id=0, has_side_effects=True, vmem_limit_bytes=60 << 20),
    )(members, layer_mats, biases, norm_gains, edge_blocks, edge_shift)
    return final_state, mean.astype(f32)


def solution(mesh):
    placed = (
        P(("section", "ens"), "dom", None),
        P("section", None, None, None),
        P("section", None, None),
        P("section", None, None),
        P("dom", None),
        P("dom", None),
    )
    return jax.shard_map(
        on_device,
        mesh=mesh,
        in_specs=placed,
        out_specs=(P(("section", "ens"), "dom", None), P("dom", None)),
        check_vma=False,
    )
```

```python
import jax
import jax.numpy as jnp
from jax import lax
from jax.experimental import pallas as pl
from jax.experimental.pallas import tpu as pltpu
from jax.sharding import PartitionSpec as P

BLK = 128
EPSILON = 1e-05
CHUNKS = 4
LANES = 128
MESH = pl.DeviceIdType.MESH


def shifted(axis, by):
    devices = lax.axis_size(axis)
    return lax.rem(lax.axis_index(axis) + by + devices, devices)


def mm(a, b):
    return jnp.dot(a, b, preferred_element_type=jnp.float32)


def centred(w):
    w = w.astype(jnp.float32)
    return (w - jnp.mean(w, axis=-1, keepdims=True)).astype(jnp.bfloat16)


def twice_half_silu(u):
    return u + u * jnp.tanh(u)


def kernel(
    members, mats, bias_in, gain_in, blocks_in, shifts_in,
    final_ref, mean_ref,
    bias, gain, blocks, shifts, w, st_in, st_out, own, halo, spread, recv_term, node_term, hid, fin, acc, acc_in, mean_b,
    small_sem, w_sem, init_send, st_sem, st_send, halo_sem, halo_send, fin_sem,
    acc_sem, acc_send, mean_sem, mean_send, out_sem, go_sem, turn_sem,
):
    sections = lax.axis_size("section")
    units = sections
    s = lax.axis_index("section")
    e = lax.axis_index("ens")
    width = members.shape[-1]
    rows = BLK // CHUNKS
    slots = 6
    last = sections - 1
    pieces = width // LANES

    d = lax.axis_index("dom")
    after = (lax.rem(s + 1, sections), d, e)
    beside = [(s, shifted("dom", by), e) for by in (1, -1)]

    def chunk(j):
        return pl.ds(j * rows, rows)

    loads = [pltpu.make_async_copy(mats.at[0, i], w.at[i], w_sem.at[i]) for i in range(6)]
    small = [
        pltpu.make_async_copy(a, b, small_sem.at[i])
        for i, (a, b) in enumerate(((blocks_in, blocks), (shifts_in, shifts), (bias_in, bias), (gain_in, gain)))
    ]
    for copy in [loads[0]] + small + [loads[i] for i in (1, 3, 2, 4, 5)]:
        copy.start()

    barrier = pltpu.get_barrier_semaphore()
    for by in range(1, sections):
        pl.semaphore_signal(barrier, inc=1, device_id={"section": shifted("section", by)}, device_id_type=MESH)
    for by in (1, -1):
        pl.semaphore_signal(barrier, inc=1, device_id={"dom": shifted("dom", by)}, device_id_type=MESH)
    pl.semaphore_signal(barrier, inc=1, device_id={"ens": 1 - e}, device_id_type=MESH)
    for copy in small:
        copy.wait()
    for i in (0, 1, 3):
        loads[i].wait()
        w[i] = w[i] * jnp.bfloat16(0.5)
    pl.semaphore_wait(barrier, sections + 2)

    def init_copy(j):
        return pltpu.make_async_remote_copy(
            members.at[0, chunk(j)], st_in.at[s, chunk(j)], init_send.at[j], st_sem.at[s, j],
            device_id={"section": 0}, device_id_type=MESH)

    def init_local(j):
        return pltpu.make_async_copy(members.at[0, chunk(j)], st_in.at[0, chunk(j)], st_sem.at[0, j])

    def state_copy(m, j):
        return pltpu.make_async_remote_copy(
            st_out.at[m, chunk(j)], st_in.at[m, chunk(j)], st_send.at[m, j], st_sem.at[m, j],
            device_id=after, device_id_type=MESH)

    def final_copy(m, j):
        return pltpu.make_async_remote_copy(
            st_out.at[m, chunk(j)], fin.at[chunk(j)], st_send.at[m, j], fin_sem.at[j],
            device_id=(m, d, e), device_id_type=MESH)

    def halo_copy(m, side, j):
        return pltpu.make_async_remote_copy(
            own.at[m, chunk(j)], halo.at[m, side, chunk(j)], halo_send.at[m], halo_sem.at[m],
            device_id=beside[side], device_id_type=MESH)

    relay = sections // 2

    @pl.when(jnp.logical_and(s > 1, s <= relay))
    def _():
        pl.semaphore_wait(go_sem, 1)

    @pl.when(s != 0)
    def _():
        for j in range(CHUNKS):
            init_copy(j).start()

    @pl.when(jnp.logical_and(s > 0, s < relay))
    def _():
        init_copy(0).wait_send()
        pl.semaphore_signal(go_sem, inc=1, device_id={"section": s + 1}, device_id_type=MESH)

    @pl.when(s == 0)
    def _():
        for j in range(CHUNKS):
            init_local(j).start()


    def put_spread(parity, block, j, values):
        values = values.astype(jnp.float32)
        for c in range(pieces):
            part = values[:, c * LANES:(c + 1) * LANES]
            spread[parity, block, c, pl.ds(j * rows, rows), :] = part
            spread[parity, block, c, pl.ds(BLK + j * rows, rows), :] = part

    def enter(m):
        parity = lax.rem(m, 2)
        for j in range(CHUNKS):
            pltpu.make_async_copy(st_in.at[m, chunk(j)], st_in.at[m, chunk(j)], st_sem.at[m, j]).wait()
            terms = mm(st_in[m, chunk(j)], w[0]).astype(jnp.bfloat16)
            own[m, chunk(j)] = terms
            for side in range(2):
                halo_copy(m, side, j).start()
            put_spread(parity, 1, j, terms)
        state = st_in[m]
        recv_term[parity] = mm(state, w[1]) + 0.5 * bias[0, 0:1]
        node_term[parity] = mm(state, w[3]) + 0.5 * bias[0, 1:2]

    def finish(m):
        parity = lax.rem(m, 2)
        pltpu.make_async_copy(halo.at[m], halo.at[m], halo_sem.at[m]).wait()
        for j in range(CHUNKS):
            for side in range(2):
                put_spread(parity, 2 * side, j, halo[m, side, chunk(j)])
        for k in range(slots):
            block = blocks[0, k]
            for c in range(pieces):
                lanes = slice(c * LANES, (c + 1) * LANES)
                u = spread[parity, block, c, pl.ds(shifts[0, k], BLK), :] + recv_term[parity, :, lanes]
                hid[pl.ds(k * BLK, BLK), lanes] = twice_half_silu(u).astype(jnp.bfloat16)
        edge = mm(hid[...], w[2])
        total = None
        for k in range(slots):
            part = edge[k * BLK:(k + 1) * BLK]
            spread_of = jnp.mean(part * part, axis=-1, keepdims=True)
            part = part * lax.rsqrt(spread_of + EPSILON)
            total = part if total is None else total + part
        messages = (total * gain[0, 0:1]).astype(jnp.bfloat16)
        u = mm(messages, w[4]) + node_term[parity]
        out = mm(twice_half_silu(u).astype(jnp.bfloat16), w[5])
        spread_of = jnp.mean(out * out, axis=-1, keepdims=True)
        state = st_in[m].astype(jnp.float32)
        state = (state + out * lax.rsqrt(spread_of + EPSILON) * gain[0, 1:2]).astype(jnp.bfloat16)
        st_out[m] = state

        @pl.when(s != last)
        def _():
            for j in range(CHUNKS):
                state_copy(m, j).start()

        @pl.when(s == last)
        def _():
            @pl.when(m != last)
            def _():
                for j in range(CHUNKS):
                    final_copy(m, j).start()

            @pl.when(m == 0)
            def _():
                acc[...] = st_out[m].astype(jnp.float32)

            @pl.when(m != 0)
            def _():
                acc[...] = acc[...] + st_out[m].astype(jnp.float32)

    @pl.when(jnp.logical_and(s == 0, e == 1))
    def _():
        pl.semaphore_wait(turn_sem, 1)

    def step(t, carry):
        @pl.when(t < units)
        def _():
            enter(t)

        @pl.when(t == 0)
        def _():
            for i in (2, 5):
                loads[i].wait()
                w[i] = centred(w[i])
            loads[4].wait()
            w[4] = w[4] * jnp.bfloat16(0.5)

            @pl.when(jnp.logical_and(s == 0, e == 0))
            def _():
                pl.semaphore_signal(turn_sem, inc=1, device_id={"ens": 1 - e}, device_id_type=MESH)

        @pl.when(t > 0)
        def _():
            finish(t - 1)

        return carry

    lax.fori_loop(0, units + 1, step, 0)

    half = BLK // 2
    mine = pl.ds(pl.multiple_of(e * half, half), half)
    theirs = pl.ds(pl.multiple_of((1 - e) * half, half), half)

    def mean_out(m, slot):
        return pltpu.make_async_remote_copy(
            mean_b.at[mine], mean_b.at[mine], mean_send.at[slot], mean_sem.at[0],
            device_id={"section": m}, device_id_type=MESH)

    mean_peer = pltpu.make_async_remote_copy(
        mean_b.at[mine], mean_b.at[mine], mean_send.at[sections - 1], mean_sem.at[1],
        device_id={"ens": 1 - e}, device_id_type=MESH)
    acc_peer = pltpu.make_async_remote_copy(
        acc.at[theirs], acc_in, acc_send, acc_sem,
        device_id={"ens": 1 - e}, device_id_type=MESH)
    order = sorted(range(1, sections), key=lambda d: -min(d, sections - d))

    @pl.when(s == last)
    def _():
        acc_peer.start()
        acc_peer.wait()
        mean_b[mine] = ((acc[mine] + acc_in[...]) * (1.0 / (2 * sections))).astype(jnp.bfloat16)
        for slot, d in enumerate(order):
            mean_out(lax.rem(s + d, sections), slot).start()
        mean_peer.start()
        pltpu.make_async_copy(st_out.at[last], final_ref.at[0], out_sem.at[0]).start()

    def drain(m, carry):
        pltpu.make_async_copy(halo.at[m], halo.at[m], halo_send.at[m]).wait()
        for j in range(CHUNKS):
            @pl.when(s != last)
            def _():
                state_copy(m, j).wait_send()

            @pl.when(jnp.logical_and(s == last, m != last))
            def _():
                final_copy(m, j).wait_send()
        return carry

    lax.fori_loop(0, units, drain, 0)

    @pl.when(s != 0)
    def _():
        for j in range(1, CHUNKS):
            init_copy(j).wait_send()

    @pl.when(s >= relay)
    def _():
        init_copy(0).wait_send()

    @pl.when(s == last)
    def _():
        for slot, d in enumerate(order):
            mean_out(lax.rem(s + d, sections), slot).wait_send()

    @pl.when(s != last)
    def _():
        for j in range(CHUNKS):
            pltpu.make_async_copy(fin.at[chunk(j)], fin.at[chunk(j)], fin_sem.at[j]).wait()
        pltpu.make_async_copy(fin, final_ref.at[0], out_sem.at[0]).start()
        pltpu.make_async_copy(mean_b.at[mine], mean_b.at[mine], mean_sem.at[0]).wait()
        mean_peer.start()

    pltpu.make_async_copy(mean_b.at[theirs], mean_b.at[theirs], mean_sem.at[1]).wait()
    mean_done = pltpu.make_async_copy(mean_b, mean_ref, out_sem.at[1])
    mean_done.start()
    mean_peer.wait_send()
    pltpu.make_async_copy(fin, final_ref.at[0], out_sem.at[0]).wait()
    mean_done.wait()


def hand_out(state_in, mean_in, state_out, mean_out, narrow, wide, sems):
    state = pltpu.make_async_copy(state_in, state_out, sems.at[0])
    taken = pltpu.make_async_copy(mean_in, narrow, sems.at[1])
    given = pltpu.make_async_copy(wide, mean_out, sems.at[2])
    taken.start()
    state.start()
    taken.wait()
    wide[...] = narrow[...].astype(jnp.float32)
    given.start()
    state.wait()
    given.wait()


def on_device(members, layer_mats, biases, norm_gains, edge_blocks, edge_shift):
    sections = lax.axis_size("section")
    width = members.shape[-1]
    bf16, f32 = jnp.bfloat16, jnp.float32
    dma = pltpu.SemaphoreType.DMA
    anywhere = pl.BlockSpec(memory_space=pl.ANY)
    final_state, mean = pl.pallas_call(
        kernel,
        out_shape=(
            jax.ShapeDtypeStruct((1, BLK, width), bf16),
            jax.ShapeDtypeStruct((BLK, width), bf16),
        ),
        in_specs=[anywhere] * 6,
        out_specs=(anywhere, anywhere),
        scratch_shapes=[
            pltpu.VMEM((1, 2, width), f32),
            pltpu.VMEM((1, 2, width), f32),
            pltpu.SMEM((1, 6), jnp.int32),
            pltpu.SMEM((1, 6), jnp.int32),
            pltpu.VMEM((6, width, width), bf16),
            pltpu.VMEM((sections, BLK, width), bf16),
            pltpu.VMEM((sections, BLK, width), bf16),
            pltpu.VMEM((sections, BLK, width), bf16),
            pltpu.VMEM((sections, 2, BLK, width), bf16),
            pltpu.VMEM((2, 3, width // LANES, 2 * BLK, LANES), f32),
            pltpu.VMEM((2, BLK, width), f32),
            pltpu.VMEM((2, BLK, width), f32),
            pltpu.VMEM((6 * BLK, width), bf16),
            pltpu.VMEM((BLK, width), bf16),
            pltpu.VMEM((BLK, width), f32),
            pltpu.VMEM((BLK // 2, width), f32),
            pltpu.VMEM((BLK, width), bf16),
            dma((4,)),
            dma((6,)),
            dma((CHUNKS,)),
            dma((sections, CHUNKS)),
            dma((sections, CHUNKS)),
            dma((sections,)),
            dma((sections,)),
            dma((CHUNKS,)),
            dma,
            dma,
            dma((2,)),
            dma((sections,)),
            dma((2,)),
            pltpu.SemaphoreType.REGULAR,
            pltpu.SemaphoreType.REGULAR,
        ],
        compiler_params=pltpu.CompilerParams(
            collective_id=0, has_side_effects=True, vmem_limit_bytes=60 << 20),
    )(members, layer_mats, biases, norm_gains, edge_blocks, edge_shift)
    return pl.pallas_call(
        hand_out,
        out_shape=(
            jax.ShapeDtypeStruct((1, BLK, width), bf16),
            jax.ShapeDtypeStruct((BLK, width), f32),
        ),
        in_specs=[anywhere] * 2,
        out_specs=(anywhere, anywhere),
        scratch_shapes=[
            pltpu.VMEM((BLK, width), bf16),
            pltpu.VMEM((BLK, width), f32),
            dma((3,)),
        ],
        compiler_params=pltpu.CompilerParams(vmem_limit_bytes=60 << 20),
    )(final_state, mean)


def solution(mesh):
    placed = (
        P(("section", "ens"), "dom", None),
        P("section", None, None, None),
        P("section", None, None),
        P("section", None, None),
        P("dom", None),
        P("dom", None),
    )
    return jax.shard_map(
        on_device,
        mesh=mesh,
        in_specs=placed,
        out_specs=(P(("section", "ens"), "dom", None), P("dom", None)),
        check_vma=False,
    )
```
